32 devices in a mesh: grp: 2 (over y), lon: 4 (over z), lat: 2 (over x), ch: 2 (over core).
Axes of the slice: x: 2, y: 2, z: 4, core: 2. Of those that a mesh axis runs over, the one named last changes fastest.
Arguments:
- features: bfloat16 [96, 256, 256], P(('grp', 'lat'), 'lon', 'ch'), parts along dimension 0, may hold values from -6 to 6
- dilation_rates: int32 [5], replicated, may hold values from 1 to 21, as said below
- branch_weight: bfloat16 [5, 3, 3, 256, 256], P(None, None, None, None, 'ch'), may hold values from -0.125 to 0.125
- branch_bias: float32 [5, 256], P(None, 'ch'), may hold values from -3 to 3
- merge_weight: bfloat16 [5, 256, 256], P(None, 'ch'), may hold values from -0.15625 to 0.15625
- cotangent: bfloat16 [96, 256, 256], P(('grp', 'lat'), 'lon', 'ch'), parts along dimension 0, may hold values from -6 to 6
Outputs:
- merged_out: bfloat16 [96, 256, 256], P(('grp', 'lat'), 'lon', 'ch'), parts along dimension 0
- feature_grad: bfloat16 [96, 256, 256], P(('grp', 'lat'), 'lon', 'ch'), parts along dimension 0
The draws below stay inside these ranges and needn't reach their ends.
There are 2 independent parts, one for each index of `grp`. The reference program is written for one: setup_inputs(seed, part) draws one part's arguments, and reference() takes and returns one part's arrays. A program takes and returns all parts, laid end to end along the dimension named above; an argument that names none is the same for every part. Nothing has to cross between parts.
Inputs may be any that keep to these rules, and one draw needn't show every extreme that they name: `dilation_rates`: one branch has rate exactly 21.
All inputs are finite; a program needn't handle non-finite values.
Results may differ from the reference program's by a relative error of at most 0.005.
Values may be sent and summed in bfloat16 or wider, within the bound.
A program may use at most 192 MiB of HBM per device.

```python
import jax
import jax.numpy as jnp
from jax import lax

C = 256
BRANCHES = 5
RMAX = 21
NLAT = 48
NLON = 256


def draw_dilation_rates(key, part):
    first_key, second_key = jax.random.split(jax.random.fold_in(key, 17))
    values_drawn = jax.random.randint(first_key, (BRANCHES,), 1, RMAX + 1)
    position = jax.random.randint(second_key, (), 0, BRANCHES)
    return jnp.where(jnp.arange(BRANCHES) == position, RMAX, values_drawn).astype(jnp.int32)


def steps_of(own_key, shape, cuts, least, largest):
    gain = 1.0
    for dim, shards_of in cuts:
        steps = jax.random.uniform(jax.random.fold_in(jax.random.fold_in(own_key, 6), dim), (shards_of,), jnp.float32, least / len(cuts), largest / len(cuts))
        gain = gain * jnp.repeat(jnp.exp(steps), shape[dim] // shards_of).reshape((-1,) + (1,) * (len(shape) - 1 - dim))
    return gain


def centred(key, shape, spread, most, pieces=(), held_as=jnp.bfloat16):
    array = jax.random.normal(key, shape, jnp.float32) * spread
    if len(pieces) > 0:
        array = steps_of(key, shape, pieces, -0.22, 0.18) * array
    return jnp.clip(array, min=-most, max=most).astype(held_as)


def setup_inputs(seed: int = 0, part: int = 0) -> dict:
    streams_of = jax.random.split(jax.random.key(seed), 7)
    part_splits = jax.random.split(jax.random.fold_in(streams_of[6], part), 7)
    features = centred(part_splits[0], (NLAT, NLON, C), 1.0, 6.0, ((0, 2), (1, 4), (2, 2)))
    dilation_rates = draw_dilation_rates(jax.random.fold_in(streams_of[6], 71), part)
    branch_weight = centred(streams_of[2], (BRANCHES, 3, 3, C, C), (9 * C) ** -0.5, 0.125, ((4, 2),))
    branch_bias = centred(streams_of[3], (BRANCHES, C), 0.5, 3.0, ((1, 2),), jnp.float32)
    merge_weight = centred(streams_of[4], (BRANCHES, C, C), (BRANCHES * C) ** -0.5, 0.15625, ((1, 2),))
    cotangent = centred(part_splits[5], (NLAT, NLON, C), 1.0, 6.0, ((0, 2), (1, 4), (2, 2)))
    return dict(features=features, dilation_rates=dilation_rates, branch_weight=branch_weight, branch_bias=branch_bias, merge_weight=merge_weight, cotangent=cotangent)


def wrap_pad(field, reach):
    field = jnp.pad(field, ((reach, reach), (0, 0), (0, 0)))
    return jnp.concatenate([field[:, -reach:], field, field[:, :reach]], axis=1)

def silu_grad(preact):
    sigma = jax.nn.sigmoid(preact)
    return sigma * (1.0 + preact * (1.0 - sigma))

def reference(features, dilation_rates, branch_weight, branch_bias, merge_weight, cotangent):
    lat_total, lon_total, channels = features.shape
    cells = lat_total * lon_total
    padded = wrap_pad(features, RMAX)
    merged_total = jnp.zeros((cells, channels), jnp.float32)
    preacts = []
    for b in range(BRANCHES):
        spacing = dilation_rates[b].astype(jnp.int32)
        total = jnp.zeros((cells, channels), jnp.float32)
        for i in range(3):
            for j in range(3):
                start_row = (RMAX + spacing * (i - 1)).astype(jnp.int32)
                start_col = (RMAX + spacing * (j - 1)).astype(jnp.int32)
                window = lax.dynamic_slice(padded, (start_row, start_col, jnp.int32(0)), (lat_total, lon_total, channels))
                total = total + jnp.dot(window.reshape(cells, channels), branch_weight[b, i, j], preferred_element_type=jnp.float32)
        preact = total + branch_bias[b]
        activated = jax.nn.silu(preact).astype(jnp.bfloat16)
        merged_total = merged_total + jnp.dot(activated, merge_weight[b], preferred_element_type=jnp.float32)
        preacts.append(preact)
    merged_out = merged_total.astype(jnp.bfloat16).reshape(lat_total, lon_total, channels)
    flat_cot = cotangent.reshape(cells, channels)
    grad_total = jnp.zeros((cells, channels), jnp.float32)
    for b in range(BRANCHES):
        spacing = dilation_rates[b].astype(jnp.int32)
        dact = jnp.dot(flat_cot, merge_weight[b].T, preferred_element_type=jnp.float32)
        dpre = (dact * silu_grad(preacts[b])).astype(jnp.bfloat16)
        padded_grad = wrap_pad(dpre.reshape(lat_total, lon_total, channels), RMAX)
        for i in range(3):
            for j in range(3):
                start_row = (RMAX - spacing * (i - 1)).astype(jnp.int32)
                start_col = (RMAX - spacing * (j - 1)).astype(jnp.int32)
                window = lax.dynamic_slice(padded_grad, (start_row, start_col, jnp.int32(0)), (lat_total, lon_total, channels))
                grad_total = grad_total + jnp.dot(window.reshape(cells, channels), branch_weight[b, i, j].T, preferred_element_type=jnp.float32)
    feature_grad = grad_total.astype(jnp.bfloat16).reshape(lat_total, lon_total, channels)
    return (merged_out, feature_grad)
```

```python
import functools

import jax
import jax.numpy as jnp
from jax import lax
from jax.experimental import pallas as pl
from jax.experimental.pallas import tpu as pltpu
from jax.sharding import PartitionSpec as P

BRANCHES = 5
RMAX = 21
PADL = 24
LANES = 128
MESH = pl.DeviceIdType.MESH
ROW_CHUNK = 8

SIDES = ((-1, 0), (1, 0), (0, -1), (0, 1), (-1, -1), (-1, 1), (1, -1), (1, 1))


def opposite(k):
    return SIDES.index((-SIDES[k][0], -SIDES[k][1]))


def strip_rows(rows):
    return (rows * RMAX + 15) // 16 * 16


class Where:
    def __init__(self, n_lat, n_lon):
        self.grp = lax.axis_index("grp")
        self.lon = lax.axis_index("lon")
        self.lat = lax.axis_index("lat")
        self.ch = lax.axis_index("ch")
        self.n_lat, self.n_lon = n_lat, n_lon
        self.up = self.lat > 0
        self.down = self.lat < n_lat - 1

    def sibling(self):
        return (self.grp, self.lon, self.lat, 1 - self.ch)

    def side(self, k):
        dlat, dlon = SIDES[k]
        lon = lax.rem(self.lon + dlon + self.n_lon, self.n_lon) if dlon else self.lon
        return (self.grp, lon, self.lat + dlat, self.ch)

    def when(self, k, body):
        dlat = SIDES[k][0]
        if dlat == 0:
            body()
        else:
            pl.when(self.up if dlat < 0 else self.down)(body)

    def barrier(self):
        sem = pltpu.get_barrier_semaphore()
        pl.semaphore_signal(sem, inc=1, device_id=self.sibling(), device_id_type=MESH)
        for k in range(8):
            self.when(
                k,
                lambda k=k: pl.semaphore_signal(
                    sem, inc=1, device_id=self.side(k), device_id_type=MESH
                ),
            )
        pl.semaphore_wait(
            sem, 3 + 3 * self.up.astype(jnp.int32) + 3 * self.down.astype(jnp.int32)
        )


def gather_kernel(n_lat, n_lon, rows, feat, cot, left, right, *refs):
    pieces = refs[:8]
    full_feat, full_cot = refs[8:10]
    send, recv, send2, recv2, local = refs[10:]
    at = Where(n_lat, n_lon)
    me = at.ch
    at.barrier()

    def source(k):
        dlat, dlon = SIDES[k]
        if dlon < 0:
            return left
        if dlon > 0:
            return right
        return feat.at[pl.ds(0, RMAX)] if dlat < 0 else feat.at[pl.ds(rows - RMAX, RMAX)]

    def to_side(k):
        return pltpu.make_async_remote_copy(
            source(k),
            pieces[opposite(k)].at[me],
            send.at[k],
            recv.at[opposite(k)],
            device_id=at.side(k),
            device_id_type=MESH,
        )

    def forward(k):
        return pltpu.make_async_remote_copy(
            pieces[k].at[me],
            pieces[k].at[me],
            send2.at[k],
            recv2.at[k],
            device_id=at.sibling(),
            device_id_type=MESH,
        )

    order = (4, 5, 6, 7, 0, 1, 2, 3)
    for k in order:
        at.when(k, lambda k=k: to_side(k).start())
    own = []
    for n, (src, dst) in enumerate(((feat, full_feat), (cot, full_cot))):
        own.append(
            pltpu.make_async_remote_copy(
                src,
                dst.at[me],
                send2.at[8 + n],
                recv2.at[8 + n],
                device_id=at.sibling(),
                device_id_type=MESH,
            )
        )
        own[-1].start()
    copies = []
    for n, (src, dst) in enumerate(((feat, full_feat), (cot, full_cot))):
        copies.append(pltpu.make_async_copy(src, dst.at[me], local.at[n]))
        copies[-1].start()

    def arrive(k):
        pltpu.make_async_remote_copy(
            pieces[k].at[me],
            pieces[k].at[me],
            send.at[k],
            recv.at[k],
            device_id=at.sibling(),
            device_id_type=MESH,
        ).wait_recv()
        forward(k).start()

    for k in (2, 3, 0, 1, 4, 5, 6, 7):
        at.when(k, lambda k=k: arrive(k))

    def other_arrives(k):
        pltpu.make_async_remote_copy(
            pieces[k].at[1 - me],
            pieces[k].at[1 - me],
            send2.at[k],
            recv2.at[k],
            device_id=at.sibling(),
            device_id_type=MESH,
        ).wait_recv()
        forward(k).wait_send()
        to_side(k).wait_send()

    for k in range(8):
        at.when(k, lambda k=k: other_arrives(k))
    for n, dst in enumerate((full_feat, full_cot)):
        own[n].wait_send()
        pltpu.make_async_remote_copy(
            dst.at[1 - me],
            dst.at[1 - me],
            send2.at[8 + n],
            recv2.at[8 + n],
            device_id=at.sibling(),
            device_id_type=MESH,
        ).wait_recv()
        copies[n].wait()


def head_kernel(
    rows, cols, info, weight, bias, merge, feat, cot, p0, p1, p2, p3, p4, p5, p6, p7,
    m_out, c_out, g0, g1, g2, g3, g4, g5, g6, g7, padded, total, merged, strip,
):
    b = pl.program_id(0)
    pieces = (p0, p1, p2, p3, p4, p5, p6, p7)
    grads = (g0, g1, g2, g3, g4, g5, g6, g7)
    all_rows = rows + 2 * RMAX
    has_up, has_down = info[BRANCHES] > 0, info[BRANCHES + 1] > 0
    right_col = PADL + cols
    near = rows * RMAX

    @pl.when(b == 0)
    def _():
        for c in range(2):
            padded[c, RMAX : RMAX + rows, PADL:right_col, :] = feat[c].astype(jnp.float32)
            for k in range(8):
                dlat, dlon = SIDES[k]
                top = {-1: 0, 0: RMAX, 1: RMAX + rows}[dlat]
                count = rows if dlat == 0 else RMAX
                skip = rows - RMAX if dlat < 0 else 0
                if dlon == 0:
                    lo, hi = PADL, right_col
                elif dlon < 0:
                    lo, hi = PADL - RMAX, PADL
                else:
                    lo, hi = right_col, right_col + RMAX

                def fill(k=k, c=c, top=top, count=count, skip=skip, lo=lo, hi=hi, dlon=dlon):
                    if dlon == 0:
                        padded[c, top : top + count, lo:hi, :] = pieces[k][c].astype(jnp.float32)
                    else:
                        strip[...] = pieces[k][c].astype(jnp.float32)
                        for n in range(count):
                            start = (skip + n) * RMAX
                            padded[c, top + n, lo:hi, :] = strip[start : start + RMAX, :]

                if dlat == 0:
                    fill()
                else:
                    there = has_up if dlat < 0 else has_down
                    pl.when(there)(fill)

                    @pl.when(jnp.logical_not(there))
                    def _(c=c, top=top, count=count, lo=lo, hi=hi):
                        padded[c, top : top + count, lo:hi, :] = jnp.zeros(
                            (count, hi - lo, LANES), jnp.float32
                        )
        total[...] = jnp.zeros_like(total)
        merged[...] = jnp.zeros_like(merged)

    rate = info[b]
    cells = ROW_CHUNK * cols

    def chunk(n, _):
        row = n * ROW_CHUNK
        taps = []
        for i in range(3):
            for j in range(3):
                for c in range(2):
                    tap = padded[
                        c,
                        pl.ds(row + RMAX + rate * (i - 1), ROW_CHUNK),
                        pl.ds(PADL + rate * (j - 1), cols),
                        :,
                    ]
                    taps.append(tap.reshape(cells, LANES).astype(jnp.bfloat16))
        preact = jnp.dot(
            jnp.concatenate(taps, axis=1),
            weight[0].reshape(9 * 2 * LANES, LANES),
            preferred_element_type=jnp.float32,
        )
        preact = preact + bias[0]
        sigma = 1.0 / (1.0 + jnp.exp(-preact))
        activated = (preact * sigma).astype(jnp.bfloat16)
        here = pl.ds(pl.multiple_of(row * cols, cells), cells)
        merged[here, :] += jnp.dot(activated, merge[0], preferred_element_type=jnp.float32)
        own_cot = jnp.concatenate(
            [cot[c, pl.ds(row, ROW_CHUNK)].reshape(cells, LANES) for c in range(2)], axis=1
        )
        dact = lax.dot_general(
            own_cot, merge[0], (((1,), (1,)), ((), ())), preferred_element_type=jnp.float32
        )
        dpre = (dact * (sigma * (1.0 + preact * (1.0 - sigma)))).astype(jnp.bfloat16)
        for i in range(3):
            for j in range(3):
                part = lax.dot_general(
                    dpre,
                    weight[0, i, j],
                    (((1,), (1,)), ((), ())),
                    preferred_element_type=jnp.float32,
                )
                for c in range(2):
                    total[
                        c,
                        pl.ds(row + RMAX + rate * (i - 1), ROW_CHUNK),
                        pl.ds(PADL + rate * (j - 1), cols),
                        :,
                    ] += part[:, c * LANES : (c + 1) * LANES].reshape(ROW_CHUNK, cols, LANES)
        return 0

    lax.fori_loop(0, rows // ROW_CHUNK, chunk, 0)

    @pl.when(b == BRANCHES - 1)
    def _():
        for c in range(2):
            m_out[c] = (
                merged[:, c * LANES : (c + 1) * LANES]
                .astype(jnp.bfloat16)
                .reshape(rows, cols, LANES)
            )
            c_out[c] = total[c, RMAX : RMAX + rows, PADL:right_col, :].astype(jnp.bfloat16)
            for k in range(8):
                dlat, dlon = SIDES[k]
                top = {-1: 0, 0: RMAX, 1: RMAX + rows}[dlat]
                count = rows if dlat == 0 else RMAX
                skip = rows - RMAX if dlat < 0 else 0
                if dlon == 0:
                    grads[k][c] = total[c, top : top + count, PADL:right_col, :].astype(
                        jnp.bfloat16
                    )
                    continue
                lo = PADL - RMAX if dlon < 0 else right_col
                strip[...] = jnp.zeros_like(strip)
                for n in range(count):
                    start = (skip + n) * RMAX
                    strip[start : start + RMAX, :] = total[c, top + n, lo : lo + RMAX, :]
                grads[k][c] = strip[...].astype(jnp.bfloat16)


def scatter_kernel(n_lat, n_lon, rows, cols, m_part, c_part, *refs):
    parts = refs[:8]
    m_out, g_out = refs[8:10]
    from_sib = refs[10:18]
    staged = refs[18:26]
    landed = refs[26:34]
    m_sib, c_sib, acc, strip, send, recv, send2, recv2 = refs[34:]
    at = Where(n_lat, n_lon)
    me = at.ch
    at.barrier()

    def to_sibling(src, dst, n):
        return pltpu.make_async_remote_copy(
            src.at[1 - me], dst, send2.at[n], recv2.at[n],
            device_id=at.sibling(), device_id_type=MESH,
        )

    def to_side(k):
        return pltpu.make_async_remote_copy(
            staged[k], landed[opposite(k)], send.at[k], recv.at[opposite(k)],
            device_id=at.side(k), device_id_type=MESH,
        )

    order = (4, 5, 6, 7, 0, 1, 2, 3)
    for k in order:
        at.when(k, lambda k=k: to_sibling(parts[k], from_sib[k], k).start())
    to_sibling(c_part, c_sib, 8).start()
    to_sibling(m_part, m_sib, 9).start()

    def reduce_and_send(k):
        to_sibling(parts[k], from_sib[k], k).wait()
        staged[k][...] = (
            parts[k][me].astype(jnp.float32) + from_sib[k][...].astype(jnp.float32)
        ).astype(jnp.bfloat16)
        to_side(k).start()

    for k in order:
        at.when(k, lambda k=k: reduce_and_send(k))

    to_sibling(c_part, c_sib, 8).wait()
    acc[...] = c_part[me].astype(jnp.float32) + c_sib[...].astype(jnp.float32)
    to_sibling(m_part, m_sib, 9).wait()
    m_out[...] = (m_part[me].astype(jnp.float32) + m_sib[...].astype(jnp.float32)).astype(
        jnp.bfloat16
    )

    def arrive(k):
        dlat, dlon = SIDES[k]
        to_side(k).wait_send()
        pltpu.make_async_remote_copy(
            landed[k], landed[k], send.at[k], recv.at[k],
            device_id=at.sibling(), device_id_type=MESH,
        ).wait_recv()
        got = landed[k][...].astype(jnp.float32)
        if dlon:
            strip[(dlon + 1) // 2] += got
        elif dlat < 0:
            acc[0:RMAX] += got
        else:
            acc[rows - RMAX : rows] += got

    strip[...] = jnp.zeros_like(strip)
    for k in order:
        at.when(k, lambda k=k: arrive(k))
    for s, lo in ((0, 0), (1, cols - RMAX)):
        for n in range(rows):
            acc[n, lo : lo + RMAX, :] += strip[s, n * RMAX : (n + 1) * RMAX, :]
    g_out[...] = acc[...].astype(jnp.bfloat16)


def on_device(n_lat, n_lon, features, dilation_rates, branch_weight, branch_bias, merge_weight, cotangent):
    rows, cols, lanes = features.shape
    channels = merge_weight.shape[2]
    flat = strip_rows(rows)
    bf16, f32 = jnp.bfloat16, jnp.float32
    vmem = pl.BlockSpec(memory_space=pltpu.VMEM)
    hbm = pl.BlockSpec(memory_space=pl.ANY)

    def pack(strip):
        return jnp.pad(strip.reshape(rows * RMAX, lanes), ((0, flat - rows * RMAX), (0, 0)))

    def piece(k):
        return (RMAX, cols, lanes) if SIDES[k][1] == 0 else (flat, lanes)

    tile = jax.ShapeDtypeStruct((2, rows, cols, lanes), bf16)
    piece_pairs = [jax.ShapeDtypeStruct((2,) + piece(k), bf16) for k in range(8)]
    gathered = pl.pallas_call(
        functools.partial(gather_kernel, n_lat, n_lon, rows),
        out_shape=piece_pairs + [tile, tile],
        in_specs=[hbm] * 4,
        out_specs=[hbm] * 10,
        scratch_shapes=[
            pltpu.SemaphoreType.DMA((8,)),
            pltpu.SemaphoreType.DMA((8,)),
            pltpu.SemaphoreType.DMA((10,)),
            pltpu.SemaphoreType.DMA((10,)),
            pltpu.SemaphoreType.DMA((2,)),
        ],
        compiler_params=pltpu.CompilerParams(collective_id=0, has_side_effects=True),
        name="gather_halo",
    )(features, cotangent, pack(features[:, :RMAX]), pack(features[:, cols - RMAX :]))
    pieces, full_feat, full_cot = gathered[:8], gathered[8], gathered[9]

    lat = lax.axis_index("lat")
    info = jnp.concatenate(
        [
            dilation_rates,
            jnp.stack([lat > 0, lat < n_lat - 1]).astype(jnp.int32),
        ]
    )
    pad_cols = PADL + cols + 24
    padded_shape = (2, rows + 2 * RMAX, pad_cols, lanes)

    def whole(shape):
        return pl.BlockSpec(shape, lambda b, *_: (0,) * len(shape))

    outs = [tile, tile] + piece_pairs
    head = pl.pallas_call(
        functools.partial(head_kernel, rows, cols),
        out_shape=outs,
        grid_spec=pltpu.PrefetchScalarGridSpec(
            num_scalar_prefetch=1,
            grid=(BRANCHES,),
            in_specs=[
                pl.BlockSpec((1, 3, 3, channels, lanes), lambda b, *_: (b, 0, 0, 0, 0)),
                pl.BlockSpec((1, 1, lanes), lambda b, *_: (b, 0, 0)),
                pl.BlockSpec((1, lanes, channels), lambda b, *_: (b, 0, 0)),
                whole(tile.shape),
                whole(tile.shape),
            ]
            + [whole(s.shape) for s in piece_pairs],
            out_specs=[whole(s.shape) for s in outs],
            scratch_shapes=[
                pltpu.VMEM(padded_shape, f32),
                pltpu.VMEM(padded_shape, f32),
                pltpu.VMEM((rows * cols, channels), f32),
                pltpu.VMEM((flat, lanes), f32),
            ],
        ),
        compiler_params=pltpu.CompilerParams(vmem_limit_bytes=56 * 2**20),
        name="head",
    )(
        info,
        branch_weight,
        branch_bias.reshape(BRANCHES, 1, lanes),
        merge_weight,
        full_feat,
        full_cot,
        *pieces,
    )

    single = [pltpu.VMEM(piece(k), bf16) for k in range(8)]
    out = jax.ShapeDtypeStruct((rows, cols, lanes), bf16)
    return pl.pallas_call(
        functools.partial(scatter_kernel, n_lat, n_lon, rows, cols),
        out_shape=[out, out],
        in_specs=[vmem] * 10,
        out_specs=[vmem] * 2,
        scratch_shapes=single
        + single
        + single
        + [
            pltpu.VMEM((rows, cols, lanes), bf16),
            pltpu.VMEM((rows, cols, lanes), bf16),
            pltpu.VMEM((rows, cols, lanes), f32),
            pltpu.VMEM((2, flat, lanes), f32),
            pltpu.SemaphoreType.DMA((8,)),
            pltpu.SemaphoreType.DMA((8,)),
            pltpu.SemaphoreType.DMA((10,)),
            pltpu.SemaphoreType.DMA((10,)),
        ],
        compiler_params=pltpu.CompilerParams(
            collective_id=1, has_side_effects=True, vmem_limit_bytes=40 * 2**20
        ),
        name="scatter_halo",
    )(*head)


def solution(mesh):
    spec = P(("grp", "lat"), "lon", "ch")
    return jax.shard_map(
        functools.partial(on_device, mesh.shape["lat"], mesh.shape["lon"]),
        mesh=mesh,
        in_specs=(
            spec,
            P(),
            P(None, None, None, None, "ch"),
            P(None, "ch"),
            P(None, "ch", None),
            spec,
        ),
        out_specs=(spec, spec),
        check_vma=False,
    )
```

```python
import functools

import jax
import jax.numpy as jnp
from jax import lax
from jax.experimental import pallas as pl
from jax.experimental.pallas import tpu as pltpu
from jax.sharding import PartitionSpec as P

BRANCHES = 5
RMAX = 21
PADL = 24
LANES = 128
MESH = pl.DeviceIdType.MESH
ROW_CHUNK = 8

SIDES = ((-1, 0), (1, 0), (0, -1), (0, 1), (-1, -1), (-1, 1), (1, -1), (1, 1))


def opposite(k):
    return SIDES.index((-SIDES[k][0], -SIDES[k][1]))


def strip_rows(rows):
    return (rows * RMAX + 15) // 16 * 16


CORNER = strip_rows(RMAX)


class Where:
    def __init__(self, n_lat, n_lon):
        self.grp = lax.axis_index("grp")
        self.lon = lax.axis_index("lon")
        self.lat = lax.axis_index("lat")
        self.ch = lax.axis_index("ch")
        self.n_lat, self.n_lon = n_lat, n_lon
        self.up = self.lat > 0
        self.down = self.lat < n_lat - 1

    def sibling(self):
        return (self.grp, self.lon, self.lat, 1 - self.ch)

    def side(self, k):
        dlat, dlon = SIDES[k]
        lon = lax.rem(self.lon + dlon + self.n_lon, self.n_lon) if dlon else self.lon
        return (self.grp, lon, self.lat + dlat, self.ch)

    def when(self, k, body):
        dlat = SIDES[k][0]
        if dlat == 0:
            body()
        else:
            pl.when(self.up if dlat < 0 else self.down)(body)

    def barrier(self):
        sem = pltpu.get_barrier_semaphore()
        pl.semaphore_signal(sem, inc=1, device_id=self.sibling(), device_id_type=MESH)
        for k in range(8):
            self.when(
                k,
                lambda k=k: pl.semaphore_signal(
                    sem, inc=1, device_id=self.side(k), device_id_type=MESH
                ),
            )
        pl.semaphore_wait(
            sem, 3 + 3 * self.up.astype(jnp.int32) + 3 * self.down.astype(jnp.int32)
        )


def gather_kernel(n_lat, n_lon, rows, cols, feat, cot, *refs):
    pieces = refs[:8]
    full_feat, full_cot = refs[8:10]
    packed = refs[10:16]
    wide, strip, send, recv, send2, recv2, local = refs[16:]
    at = Where(n_lat, n_lon)
    me = at.ch
    copies = []
    for n, (src, dst) in enumerate(((feat, full_feat), (cot, full_cot))):
        copies.append(pltpu.make_async_copy(src, dst.at[me], local.at[n]))
        copies[-1].start()
    at.barrier()
    copies[0].wait()

    def source(k):
        dlat, dlon = SIDES[k]
        if dlon:
            return packed[k - 2]
        own = full_feat.at[me]
        return own.at[pl.ds(0, RMAX)] if dlat < 0 else own.at[pl.ds(rows - RMAX, RMAX)]

    def to_side(k):
        return pltpu.make_async_remote_copy(
            source(k),
            pieces[opposite(k)].at[me],
            send.at[k],
            recv.at[opposite(k)],
            device_id=at.side(k),
            device_id_type=MESH,
        )

    def forward(k):
        return pltpu.make_async_remote_copy(
            pieces[k].at[me],
            pieces[k].at[me],
            send2.at[k],
            recv2.at[k],
            device_id=at.sibling(),
            device_id_type=MESH,
        )

    for k in (0, 1):
        at.when(k, lambda k=k: to_side(k).start())
    wide[...] = full_feat[me].astype(jnp.float32)
    far = (rows - RMAX) * RMAX
    strip[...] = jnp.zeros_like(strip)
    for s, lo in ((0, 0), (1, cols - RMAX)):
        for n in range(rows):
            strip[s, n * RMAX : (n + 1) * RMAX, :] = wide[n, lo : lo + RMAX, :]
        for k in (2 + s, 4 + s, 6 + s):
            start, size = {2: (0, strip.shape[1]), 4: (0, CORNER), 6: (far, CORNER)}[k - s]
            packed[k - 2][...] = strip[s, start : start + size, :].astype(jnp.bfloat16)
            at.when(k, lambda k=k: to_side(k).start())
    own = []
    for n, full in enumerate((full_feat, full_cot)):
        if n:
            copies[n].wait()
        own.append(
            pltpu.make_async_remote_copy(
                full.at[me],
                full.at[me],
                send2.at[8 + n],
                recv2.at[8 + n],
                device_id=at.sibling(),
                device_id_type=MESH,
            )
        )
        own[-1].start()

    def arrive(k):
        pltpu.make_async_remote_copy(
            pieces[k].at[me],
            pieces[k].at[me],
            send.at[k],
            recv.at[k],
            device_id=at.sibling(),
            device_id_type=MESH,
        ).wait_recv()
        forward(k).start()

    for k in (2, 3, 0, 1, 4, 5, 6, 7):
        at.when(k, lambda k=k: arrive(k))

    def other_arrives(k):
        pltpu.make_async_remote_copy(
            pieces[k].at[1 - me],
            pieces[k].at[1 - me],
            send2.at[k],
            recv2.at[k],
            device_id=at.sibling(),
            device_id_type=MESH,
        ).wait_recv()
        forward(k).wait_send()
        to_side(k).wait_send()

    for k in range(8):
        at.when(k, lambda k=k: other_arrives(k))
    for n, dst in enumerate((full_feat, full_cot)):
        own[n].wait_send()
        pltpu.make_async_remote_copy(
            dst.at[1 - me],
            dst.at[1 - me],
            send2.at[8 + n],
            recv2.at[8 + n],
            device_id=at.sibling(),
            device_id_type=MESH,
        ).wait_recv()


def head_kernel(
    rows, cols, n_lat, info, weight, bias, merge, feat, cot, p0, p1, p2, p3, p4, p5, p6, p7,
    m_out, c_out, g0, g1, g2, g3, g4, g5, g6, g7, padded, total, merged, strip,
):
    b = pl.program_id(0)
    pieces = (p0, p1, p2, p3, p4, p5, p6, p7)
    grads = (g0, g1, g2, g3, g4, g5, g6, g7)
    all_rows = rows + 2 * RMAX
    lat = lax.axis_index("lat")
    has_up, has_down = lat > 0, lat < n_lat - 1
    right_col = PADL + cols

    @pl.when(b == 0)
    def _():
        for c in range(2):
            padded[c, RMAX : RMAX + rows, PADL:right_col, :] = feat[c].astype(jnp.float32)
            for k in range(8):
                dlat, dlon = SIDES[k]
                top = {-1: 0, 0: RMAX, 1: RMAX + rows}[dlat]
                count = rows if dlat == 0 else RMAX
                if dlon == 0:
                    lo, hi = PADL, right_col
                elif dlon < 0:
                    lo, hi = PADL - RMAX, PADL
                else:
                    lo, hi = right_col, right_col + RMAX

                def fill(k=k, c=c, top=top, count=count, lo=lo, hi=hi, dlat=dlat, dlon=dlon):
                    if dlon == 0:
                        padded[c, top : top + count, lo:hi, :] = pieces[k][c].astype(jnp.float32)
                    else:
                        size = CORNER if dlat else strip.shape[0]
                        strip[0:size, :] = pieces[k][c].astype(jnp.float32)
                        for n in range(count):
                            start = n * RMAX
                            padded[c, top + n, lo:hi, :] = strip[start : start + RMAX, :]

                if dlat == 0:
                    fill()
                else:
                    there = has_up if dlat < 0 else has_down
                    pl.when(there)(fill)

                    @pl.when(jnp.logical_not(there))
                    def _(c=c, top=top, count=count, lo=lo, hi=hi):
                        padded[c, top : top + count, lo:hi, :] = jnp.zeros(
                            (count, hi - lo, LANES), jnp.float32
                        )
        total[...] = jnp.zeros_like(total)
        merged[...] = jnp.zeros_like(merged)

    rate = info[b]
    cells = ROW_CHUNK * cols

    def chunk(n, _):
        row = n * ROW_CHUNK
        taps = []
        for i in range(3):
            for j in range(3):
                for c in range(2):
                    tap = padded[
                        c,
                        pl.ds(row + RMAX + rate * (i - 1), ROW_CHUNK),
                        pl.ds(PADL + rate * (j - 1), cols),
                        :,
                    ]
                    taps.append(tap.reshape(cells, LANES).astype(jnp.bfloat16))
        preact = jnp.dot(
            jnp.concatenate(taps, axis=1),
            weight[0].reshape(9 * 2 * LANES, LANES),
            preferred_element_type=jnp.float32,
        )
        preact = preact + bias[pl.ds(b, 1), :]
        sigma = 1.0 / (1.0 + jnp.exp(-preact))
        activated = (preact * sigma).astype(jnp.bfloat16)
        here = pl.ds(pl.multiple_of(row * cols, cells), cells)
        merged[here, :] += jnp.dot(activated, merge[0], preferred_element_type=jnp.float32)
        own_cot = jnp.concatenate(
            [cot[c, pl.ds(row, ROW_CHUNK)].reshape(cells, LANES) for c in range(2)], axis=1
        )
        dact = lax.dot_general(
            own_cot, merge[0], (((1,), (1,)), ((), ())), preferred_element_type=jnp.float32
        )
        dpre = (dact * (sigma * (1.0 + preact * (1.0 - sigma)))).astype(jnp.bfloat16)
        for i in range(3):
            for j in range(3):
                part = lax.dot_general(
                    dpre,
                    weight[0, i, j],
                    (((1,), (1,)), ((), ())),
                    preferred_element_type=jnp.float32,
                )
                for c in range(2):
                    total[
                        c,
                        pl.ds(row + RMAX + rate * (i - 1), ROW_CHUNK),
                        pl.ds(PADL + rate * (j - 1), cols),
                        :,
                    ] += part[:, c * LANES : (c + 1) * LANES].reshape(ROW_CHUNK, cols, LANES)
        return 0

    lax.fori_loop(0, rows // ROW_CHUNK, chunk, 0)

    @pl.when(b == BRANCHES - 1)
    def _():
        for c in range(2):
            m_out[c] = (
                merged[:, c * LANES : (c + 1) * LANES]
                .astype(jnp.bfloat16)
                .reshape(rows, cols, LANES)
            )
            c_out[c] = total[c, RMAX : RMAX + rows, PADL:right_col, :].astype(jnp.bfloat16)
            for k in range(8):
                dlat, dlon = SIDES[k]
                top = {-1: 0, 0: RMAX, 1: RMAX + rows}[dlat]
                count = rows if dlat == 0 else RMAX
                if dlon == 0:
                    grads[k][c] = total[c, top : top + count, PADL:right_col, :].astype(
                        jnp.bfloat16
                    )
                    continue
                lo = PADL - RMAX if dlon < 0 else right_col
                strip[...] = jnp.zeros_like(strip)
                for n in range(count):
                    start = n * RMAX
                    strip[start : start + RMAX, :] = total[c, top + n, lo : lo + RMAX, :]
                size = CORNER if dlat else strip.shape[0]
                grads[k][c] = strip[0:size, :].astype(jnp.bfloat16)


def scatter_kernel(n_lat, n_lon, rows, cols, m_part, c_part, *refs):
    parts = refs[:8]
    m_out, g_out = refs[8:10]
    from_sib = refs[10:18]
    staged = refs[18:26]
    landed = refs[26:34]
    m_sib, c_sib, acc, strip, send, recv, send2, recv2 = refs[34:]
    at = Where(n_lat, n_lon)
    me = at.ch
    at.barrier()

    def to_sibling(src, dst, n):
        return pltpu.make_async_remote_copy(
            src.at[1 - me], dst, send2.at[n], recv2.at[n],
            device_id=at.sibling(), device_id_type=MESH,
        )

    def to_side(k):
        return pltpu.make_async_remote_copy(
            staged[k], landed[opposite(k)], send.at[k], recv.at[opposite(k)],
            device_id=at.side(k), device_id_type=MESH,
        )

    order = (4, 5, 6, 7, 0, 1, 2, 3)
    for k in order:
        at.when(k, lambda k=k: to_sibling(parts[k], from_sib[k], k).start())
    to_sibling(c_part, c_sib, 8).start()
    to_sibling(m_part, m_sib, 9).start()

    def reduce_and_send(k):
        to_sibling(parts[k], from_sib[k], k).wait()
        staged[k][...] = (
            parts[k][me].astype(jnp.float32) + from_sib[k][...].astype(jnp.float32)
        ).astype(jnp.bfloat16)
        to_side(k).start()

    for k in order:
        at.when(k, lambda k=k: reduce_and_send(k))

    to_sibling(c_part, c_sib, 8).wait()
    acc[...] = c_part[me].astype(jnp.float32) + c_sib[...].astype(jnp.float32)
    to_sibling(m_part, m_sib, 9).wait()
    m_out[...] = (m_part[me].astype(jnp.float32) + m_sib[...].astype(jnp.float32)).astype(
        jnp.bfloat16
    )

    def arrive(k):
        dlat, dlon = SIDES[k]
        to_side(k).wait_send()
        pltpu.make_async_remote_copy(
            landed[k], landed[k], send.at[k], recv.at[k],
            device_id=at.sibling(), device_id_type=MESH,
        ).wait_recv()
        got = landed[k][...].astype(jnp.float32)
        if dlon:
            start = (rows - RMAX) * RMAX if dlat > 0 else 0
            strip[(dlon + 1) // 2, start : start + got.shape[0], :] += got
        elif dlat < 0:
            acc[0:RMAX] += got
        else:
            acc[rows - RMAX : rows] += got

    strip[...] = jnp.zeros_like(strip)
    for k in order:
        at.when(k, lambda k=k: arrive(k))
    for s, lo in ((0, 0), (1, cols - RMAX)):
        for n in range(rows):
            acc[n, lo : lo + RMAX, :] += strip[s, n * RMAX : (n + 1) * RMAX, :]
    g_out[...] = acc[...].astype(jnp.bfloat16)


def on_device(n_lat, n_lon, features, dilation_rates, branch_weight, branch_bias, merge_weight, cotangent):
    rows, cols, lanes = features.shape
    channels = merge_weight.shape[2]
    flat = strip_rows(rows)
    bf16, f32 = jnp.bfloat16, jnp.float32
    vmem = pl.BlockSpec(memory_space=pltpu.VMEM)
    hbm = pl.BlockSpec(memory_space=pl.ANY)

    def piece(k):
        dlat, dlon = SIDES[k]
        if dlon == 0:
            return (RMAX, cols, lanes)
        return (CORNER if dlat else flat, lanes)

    tile = jax.ShapeDtypeStruct((2, rows, cols, lanes), bf16)
    piece_pairs = [jax.ShapeDtypeStruct((2,) + piece(k), bf16) for k in range(8)]
    gathered = pl.pallas_call(
        functools.partial(gather_kernel, n_lat, n_lon, rows, cols),
        out_shape=piece_pairs + [tile, tile],
        in_specs=[hbm] * 2,
        out_specs=[vmem] * 10,
        scratch_shapes=[pltpu.VMEM(piece(k), bf16) for k in range(2, 8)]
        + [
            pltpu.VMEM((rows, cols, lanes), f32),
            pltpu.VMEM((2, flat, lanes), f32),
            pltpu.SemaphoreType.DMA((8,)),
            pltpu.SemaphoreType.DMA((8,)),
            pltpu.SemaphoreType.DMA((10,)),
            pltpu.SemaphoreType.DMA((10,)),
            pltpu.SemaphoreType.DMA((2,)),
        ],
        compiler_params=pltpu.CompilerParams(
            collective_id=0, has_side_effects=True, vmem_limit_bytes=24 * 2**20
        ),
        name="gather_halo",
    )(features, cotangent)
    pieces, full_feat, full_cot = gathered[:8], gathered[8], gathered[9]

    pad_cols = PADL + cols + 24
    padded_shape = (2, rows + 2 * RMAX, pad_cols, lanes)

    outs = [tile, tile] + piece_pairs
    head = pl.pallas_call(
        functools.partial(head_kernel, rows, cols, n_lat),
        out_shape=outs,
        grid_spec=pltpu.PrefetchScalarGridSpec(
            num_scalar_prefetch=1,
            grid=(BRANCHES,),
            in_specs=[
                pl.BlockSpec((1, 3, 3, channels, lanes), lambda b, *_: (b, 0, 0, 0, 0)),
                vmem,
                pl.BlockSpec((1, lanes, channels), lambda b, *_: (b, 0, 0)),
            ]
            + [vmem] * 10,
            out_specs=[vmem] * 10,
            scratch_shapes=[
                pltpu.VMEM(padded_shape, f32),
                pltpu.VMEM(padded_shape, f32),
                pltpu.VMEM((rows * cols, channels), f32),
                pltpu.VMEM((flat, lanes), f32),
            ],
        ),
        compiler_params=pltpu.CompilerParams(vmem_limit_bytes=32 * 2**20),
        name="head",
    )(
        dilation_rates,
        branch_weight,
        branch_bias,
        merge_weight,
        full_feat,
        full_cot,
        *pieces,
    )

    single = [pltpu.VMEM(piece(k), bf16) for k in range(8)]
    out = jax.ShapeDtypeStruct((rows, cols, lanes), bf16)
    return pl.pallas_call(
        functools.partial(scatter_kernel, n_lat, n_lon, rows, cols),
        out_shape=[out, out],
        in_specs=[vmem] * 10,
        out_specs=[vmem] * 2,
        scratch_shapes=single
        + single
        + single
        + [
            pltpu.VMEM((rows, cols, lanes), bf16),
            pltpu.VMEM((rows, cols, lanes), bf16),
            pltpu.VMEM((rows, cols, lanes), f32),
            pltpu.VMEM((2, flat, lanes), f32),
            pltpu.SemaphoreType.DMA((8,)),
            pltpu.SemaphoreType.DMA((8,)),
            pltpu.SemaphoreType.DMA((10,)),
            pltpu.SemaphoreType.DMA((10,)),
        ],
        compiler_params=pltpu.CompilerParams(
            collective_id=1, has_side_effects=True, vmem_limit_bytes=24 * 2**20
        ),
        name="scatter_halo",
    )(*head)


def solution(mesh):
    spec = P(("grp", "lat"), "lon", "ch")
    return jax.shard_map(
        functools.partial(on_device, mesh.shape["lat"], mesh.shape["lon"]),
        mesh=mesh,
        in_specs=(
            spec,
            P(),
            P(None, None, None, None, "ch"),
            P(None, "ch"),
            P(None, "ch", None),
            spec,
        ),
        out_specs=(spec, spec),
        check_vma=False,
    )
```

```python
import functools

import jax
import jax.numpy as jnp
from jax import lax
from jax.experimental import pallas as pl
from jax.experimental.pallas import tpu as pltpu
from jax.sharding import PartitionSpec as P

BRANCHES = 5
RMAX = 21
PADL = 24
LANES = 128
MESH = pl.DeviceIdType.MESH

SIDES = ((-1, 0), (1, 0), (0, -1), (0, 1), (-1, -1), (-1, 1), (1, -1), (1, 1))


def opposite(k):
    return SIDES.index((-SIDES[k][0], -SIDES[k][1]))


def strip_rows(rows):
    return (rows * RMAX + 15) // 16 * 16


CORNER = strip_rows(RMAX)


class Where:
    def __init__(self, n_lat, n_lon):
        self.grp = lax.axis_index("grp")
        self.lon = lax.axis_index("lon")
        self.lat = lax.axis_index("lat")
        self.ch = lax.axis_index("ch")
        self.n_lat, self.n_lon = n_lat, n_lon
        self.up = self.lat > 0
        self.down = self.lat < n_lat - 1

    def sibling(self):
        return (self.grp, self.lon, self.lat, 1 - self.ch)

    def side(self, k):
        dlat, dlon = SIDES[k]
        lon = lax.rem(self.lon + dlon + self.n_lon, self.n_lon) if dlon else self.lon
        return (self.grp, lon, self.lat + dlat, self.ch)

    def when(self, k, body):
        dlat = SIDES[k][0]
        if dlat == 0:
            body()
        else:
            pl.when(self.up if dlat < 0 else self.down)(body)

    def barrier(self):
        sem = pltpu.get_barrier_semaphore()
        pl.semaphore_signal(sem, inc=1, device_id=self.sibling(), device_id_type=MESH)
        for k in range(8):
            self.when(
                k,
                lambda k=k: pl.semaphore_signal(
                    sem, inc=1, device_id=self.side(k), device_id_type=MESH
                ),
            )
        pl.semaphore_wait(
            sem, 3 + 3 * self.up.astype(jnp.int32) + 3 * self.down.astype(jnp.int32)
        )


def gather_kernel(n_lat, n_lon, rows, cols, *refs):
    owns, refs = refs[:5], refs[5:]
    pieces = refs[:8]
    fulls = refs[8:13]
    full_feat = fulls[0]
    packed = refs[13:19]
    wide, strip, send, recv, send2, recv2, local = refs[19:]
    at = Where(n_lat, n_lon)
    me = at.ch
    copies = []
    for n, (src, dst) in enumerate(zip(owns, fulls)):
        copies.append(pltpu.make_async_copy(src, dst.at[me], local.at[n]))
        copies[-1].start()
    at.barrier()
    copies[0].wait()

    def source(k):
        dlat, dlon = SIDES[k]
        if dlon:
            return packed[k - 2]
        own = full_feat.at[me]
        return own.at[pl.ds(0, RMAX)] if dlat < 0 else own.at[pl.ds(rows - RMAX, RMAX)]

    def to_side(k):
        return pltpu.make_async_remote_copy(
            source(k),
            pieces[opposite(k)].at[me],
            send.at[k],
            recv.at[opposite(k)],
            device_id=at.side(k),
            device_id_type=MESH,
        )

    def forward(k):
        return pltpu.make_async_remote_copy(
            pieces[k].at[me],
            pieces[k].at[me],
            send2.at[k],
            recv2.at[k],
            device_id=at.sibling(),
            device_id_type=MESH,
        )

    for k in (0, 1):
        at.when(k, lambda k=k: to_side(k).start())
    wide[...] = full_feat[me].astype(jnp.float32)
    far = (rows - RMAX) * RMAX
    strip[...] = jnp.zeros_like(strip)
    for s, lo in ((0, 0), (1, cols - RMAX)):
        for n in range(rows):
            strip[s, n * RMAX : (n + 1) * RMAX, :] = wide[n, lo : lo + RMAX, :]
        for k in (2 + s, 4 + s, 6 + s):
            start, size = {2: (0, strip.shape[1]), 4: (0, CORNER), 6: (far, CORNER)}[k - s]
            packed[k - 2][...] = strip[s, start : start + size, :].astype(jnp.bfloat16)
            at.when(k, lambda k=k: to_side(k).start())
    own = []
    for n, full in enumerate(fulls):
        if n:
            copies[n].wait()
        own.append(
            pltpu.make_async_remote_copy(
                full.at[me],
                full.at[me],
                send2.at[8 + n],
                recv2.at[8 + n],
                device_id=at.sibling(),
                device_id_type=MESH,
            )
        )
        own[-1].start()

    def arrive(k):
        pltpu.make_async_remote_copy(
            pieces[k].at[me],
            pieces[k].at[me],
            send.at[k],
            recv.at[k],
            device_id=at.sibling(),
            device_id_type=MESH,
        ).wait_recv()
        forward(k).start()

    for k in (2, 3, 0, 1, 4, 5, 6, 7):
        at.when(k, lambda k=k: arrive(k))

    def other_arrives(k):
        pltpu.make_async_remote_copy(
            pieces[k].at[1 - me],
            pieces[k].at[1 - me],
            send2.at[k],
            recv2.at[k],
            device_id=at.sibling(),
            device_id_type=MESH,
        ).wait_recv()
        forward(k).wait_send()
        to_side(k).wait_send()

    for k in range(8):
        at.when(k, lambda k=k: other_arrives(k))
    for n, dst in enumerate(fulls):
        own[n].wait_send()
        pltpu.make_async_remote_copy(
            dst.at[1 - me],
            dst.at[1 - me],
            send2.at[8 + n],
            recv2.at[8 + n],
            device_id=at.sibling(),
            device_id_type=MESH,
        ).wait_recv()


def head_kernel(
    rows, cols, n_lat, info, weight, bias, merge, feat, cot, p0, p1, p2, p3, p4, p5, p6, p7,
    m_out, c_out, g0, g1, g2, g3, g4, g5, g6, g7, padded, total, merged, strip,
):
    b = pl.program_id(0)
    pieces = (p0, p1, p2, p3, p4, p5, p6, p7)
    grads = (g0, g1, g2, g3, g4, g5, g6, g7)
    all_rows = rows + 2 * RMAX
    lat = lax.axis_index("lat")
    first_row = lax.axis_index("ch") * (rows // 2)
    has_up, has_down = lat > 0, lat < n_lat - 1
    right_col = PADL + cols

    @pl.when(b == 0)
    def _():
        for c in range(2):
            padded[c, RMAX : RMAX + rows, PADL:right_col, :] = feat[c].astype(jnp.float32)
            for k in range(8):
                dlat, dlon = SIDES[k]
                top = {-1: 0, 0: RMAX, 1: RMAX + rows}[dlat]
                count = rows if dlat == 0 else RMAX
                if dlon == 0:
                    lo, hi = PADL, right_col
                elif dlon < 0:
                    lo, hi = PADL - RMAX, PADL
                else:
                    lo, hi = right_col, right_col + RMAX

                def fill(k=k, c=c, top=top, count=count, lo=lo, hi=hi, dlat=dlat, dlon=dlon):
                    if dlon == 0:
                        padded[c, top : top + count, lo:hi, :] = pieces[k][c].astype(jnp.float32)
                    else:
                        size = CORNER if dlat else strip.shape[0]
                        strip[0:size, :] = pieces[k][c].astype(jnp.float32)
                        for n in range(count):
                            start = n * RMAX
                            padded[c, top + n, lo:hi, :] = strip[start : start + RMAX, :]

                if dlat == 0:
                    fill()
                else:
                    there = has_up if dlat < 0 else has_down
                    pl.when(there)(fill)

                    @pl.when(jnp.logical_not(there))
                    def _(c=c, top=top, count=count, lo=lo, hi=hi):
                        padded[c, top : top + count, lo:hi, :] = jnp.zeros(
                            (count, hi - lo, LANES), jnp.float32
                        )
        total[...] = jnp.zeros_like(total)
        merged[...] = jnp.zeros_like(merged)

    rate = info[b]
    own_rows = rows // 2
    cells = own_rows * cols
    taps = []
    for i in range(3):
        for j in range(3):
            for c in range(2):
                tap = padded[
                    c,
                    pl.ds(first_row + RMAX + rate * (i - 1), own_rows),
                    pl.ds(PADL + rate * (j - 1), cols),
                    :,
                ]
                taps.append(tap.reshape(cells, LANES).astype(jnp.bfloat16))
    kernel = jnp.concatenate(
        [weight[h, b].reshape(9 * 2 * LANES, LANES) for h in range(2)], axis=1
    )
    preact = jnp.dot(
        jnp.concatenate(taps, axis=1), kernel, preferred_element_type=jnp.float32
    )
    preact = preact + jnp.concatenate([bias[h, pl.ds(b, 1), :] for h in range(2)], axis=1)
    sigma = 1.0 / (1.0 + jnp.exp(-preact))
    activated = (preact * sigma).astype(jnp.bfloat16)
    project = jnp.concatenate([merge[h, b] for h in range(2)], axis=0)
    here = pl.ds(pl.multiple_of(first_row * cols, cells), cells)
    merged[here, :] += jnp.dot(activated, project, preferred_element_type=jnp.float32)
    own_cot = jnp.concatenate(
        [cot[c, pl.ds(first_row, own_rows)].reshape(cells, LANES) for c in range(2)], axis=1
    )
    transposed = (((1,), (1,)), ((), ()))
    dact = lax.dot_general(own_cot, project, transposed, preferred_element_type=jnp.float32)
    dpre = (dact * (sigma * (1.0 + preact * (1.0 - sigma)))).astype(jnp.bfloat16)
    for i in range(3):
        for j in range(3):
            part = lax.dot_general(
                dpre,
                jnp.concatenate([weight[h, b, i, j] for h in range(2)], axis=1),
                transposed,
                preferred_element_type=jnp.float32,
            )
            for c in range(2):
                total[
                    c,
                    pl.ds(first_row + RMAX + rate * (i - 1), own_rows),
                    pl.ds(PADL + rate * (j - 1), cols),
                    :,
                ] += part[:, c * LANES : (c + 1) * LANES].reshape(own_rows, cols, LANES)

    @pl.when(b == BRANCHES - 1)
    def _():
        for c in range(2):
            m_out[c] = (
                merged[:, c * LANES : (c + 1) * LANES]
                .astype(jnp.bfloat16)
                .reshape(rows, cols, LANES)
            )
            c_out[c] = total[c, RMAX : RMAX + rows, PADL:right_col, :].astype(jnp.bfloat16)
            for k in range(8):
                dlat, dlon = SIDES[k]
                top = {-1: 0, 0: RMAX, 1: RMAX + rows}[dlat]
                count = rows if dlat == 0 else RMAX
                if dlon == 0:
                    grads[k][c] = total[c, top : top + count, PADL:right_col, :].astype(
                        jnp.bfloat16
                    )
                    continue
                lo = PADL - RMAX if dlon < 0 else right_col
                strip[...] = jnp.zeros_like(strip)
                for n in range(count):
                    start = n * RMAX
                    strip[start : start + RMAX, :] = total[c, top + n, lo : lo + RMAX, :]
                size = CORNER if dlat else strip.shape[0]
                grads[k][c] = strip[0:size, :].astype(jnp.bfloat16)


def scatter_kernel(n_lat, n_lon, rows, cols, m_part, c_part, *refs):
    parts = refs[:8]
    m_out, g_out = refs[8:10]
    from_sib = refs[10:18]
    staged = refs[18:26]
    landed = refs[26:34]
    m_sib, c_sib, acc, strip, send, recv, send2, recv2 = refs[34:]
    at = Where(n_lat, n_lon)
    me = at.ch
    at.barrier()

    def to_sibling(src, dst, n):
        return pltpu.make_async_remote_copy(
            src.at[1 - me], dst, send2.at[n], recv2.at[n],
            device_id=at.sibling(), device_id_type=MESH,
        )

    def to_side(k):
        return pltpu.make_async_remote_copy(
            staged[k], landed[opposite(k)], send.at[k], recv.at[opposite(k)],
            device_id=at.side(k), device_id_type=MESH,
        )

    order = (4, 5, 6, 7, 0, 1, 2, 3)
    for k in order:
        at.when(k, lambda k=k: to_sibling(parts[k], from_sib[k], k).start())
    to_sibling(c_part, c_sib, 8).start()
    to_sibling(m_part, m_sib, 9).start()

    def reduce_and_send(k):
        to_sibling(parts[k], from_sib[k], k).wait()
        staged[k][...] = (
            parts[k][me].astype(jnp.float32) + from_sib[k][...].astype(jnp.float32)
        ).astype(jnp.bfloat16)
        to_side(k).start()

    for k in order:
        at.when(k, lambda k=k: reduce_and_send(k))

    to_sibling(c_part, c_sib, 8).wait()
    acc[...] = c_part[me].astype(jnp.float32) + c_sib[...].astype(jnp.float32)
    to_sibling(m_part, m_sib, 9).wait()
    m_out[...] = (m_part[me].astype(jnp.float32) + m_sib[...].astype(jnp.float32)).astype(
        jnp.bfloat16
    )

    def arrive(k):
        dlat, dlon = SIDES[k]
        to_side(k).wait_send()
        pltpu.make_async_remote_copy(
            landed[k], landed[k], send.at[k], recv.at[k],
            device_id=at.sibling(), device_id_type=MESH,
        ).wait_recv()
        got = landed[k][...].astype(jnp.float32)
        if dlon:
            start = (rows - RMAX) * RMAX if dlat > 0 else 0
            strip[(dlon + 1) // 2, start : start + got.shape[0], :] += got
        elif dlat < 0:
            acc[0:RMAX] += got
        else:
            acc[rows - RMAX : rows] += got

    strip[...] = jnp.zeros_like(strip)
    for k in order:
        at.when(k, lambda k=k: arrive(k))
    for s, lo in ((0, 0), (1, cols - RMAX)):
        for n in range(rows):
            acc[n, lo : lo + RMAX, :] += strip[s, n * RMAX : (n + 1) * RMAX, :]
    g_out[...] = acc[...].astype(jnp.bfloat16)


def on_device(n_lat, n_lon, features, dilation_rates, branch_weight, branch_bias, merge_weight, cotangent):
    rows, cols, lanes = features.shape
    channels = merge_weight.shape[2]
    flat = strip_rows(rows)
    bf16, f32 = jnp.bfloat16, jnp.float32
    vmem = pl.BlockSpec(memory_space=pltpu.VMEM)
    hbm = pl.BlockSpec(memory_space=pltpu.HBM)

    def piece(k):
        dlat, dlon = SIDES[k]
        if dlon == 0:
            return (RMAX, cols, lanes)
        return (CORNER if dlat else flat, lanes)

    tile = jax.ShapeDtypeStruct((2, rows, cols, lanes), bf16)
    piece_pairs = [jax.ShapeDtypeStruct((2,) + piece(k), bf16) for k in range(8)]
    own = (features, cotangent, branch_weight, merge_weight, branch_bias)
    gathered = pl.pallas_call(
        functools.partial(gather_kernel, n_lat, n_lon, rows, cols),
        out_shape=piece_pairs + [jax.ShapeDtypeStruct((2,) + a.shape, a.dtype) for a in own],
        in_specs=[hbm] * 5,
        out_specs=[vmem] * 13,
        scratch_shapes=[pltpu.VMEM(piece(k), bf16) for k in range(2, 8)]
        + [
            pltpu.VMEM((rows, cols, lanes), f32),
            pltpu.VMEM((2, flat, lanes), f32),
            pltpu.SemaphoreType.DMA((8,)),
            pltpu.SemaphoreType.DMA((8,)),
            pltpu.SemaphoreType.DMA((13,)),
            pltpu.SemaphoreType.DMA((13,)),
            pltpu.SemaphoreType.DMA((5,)),
        ],
        compiler_params=pltpu.CompilerParams(
            collective_id=0, has_side_effects=True, vmem_limit_bytes=24 * 2**20
        ),
        name="gather_halo",
    )(*own)
    pieces, full_feat, full_cot = gathered[:8], gathered[8], gathered[9]
    weights, merges, biases = gathered[10:]

    pad_cols = PADL + cols + 24
    padded_shape = (2, rows + 2 * RMAX, pad_cols, lanes)

    outs = [tile, tile] + piece_pairs
    head = pl.pallas_call(
        functools.partial(head_kernel, rows, cols, n_lat),
        out_shape=outs,
        grid_spec=pltpu.PrefetchScalarGridSpec(
            num_scalar_prefetch=1,
            grid=(BRANCHES,),
            in_specs=[vmem] * 13,
            out_specs=[vmem] * 10,
            scratch_shapes=[
                pltpu.VMEM(padded_shape, f32),
                pltpu.VMEM(padded_shape, f32),
                pltpu.VMEM((rows * cols, channels), f32),
                pltpu.VMEM((flat, lanes), f32),
            ],
        ),
        compiler_params=pltpu.CompilerParams(vmem_limit_bytes=32 * 2**20),
        name="head",
    )(
        dilation_rates,
        weights,
        biases,
        merges,
        full_feat,
        full_cot,
        *pieces,
    )

    single = [pltpu.VMEM(piece(k), bf16) for k in range(8)]
    out = jax.ShapeDtypeStruct((rows, cols, lanes), bf16)
    return pl.pallas_call(
        functools.partial(scatter_kernel, n_lat, n_lon, rows, cols),
        out_shape=[out, out],
        in_specs=[vmem] * 10,
        out_specs=[vmem] * 2,
        scratch_shapes=single
        + single
        + single
        + [
            pltpu.VMEM((rows, cols, lanes), bf16),
            pltpu.VMEM((rows, cols, lanes), bf16),
            pltpu.VMEM((rows, cols, lanes), f32),
            pltpu.VMEM((2, flat, lanes), f32),
            pltpu.SemaphoreType.DMA((8,)),
            pltpu.SemaphoreType.DMA((8,)),
            pltpu.SemaphoreType.DMA((10,)),
            pltpu.SemaphoreType.DMA((10,)),
        ],
        compiler_params=pltpu.CompilerParams(
            collective_id=1, has_side_effects=True, vmem_limit_bytes=24 * 2**20
        ),
        name="scatter_halo",
    )(*head)


def solution(mesh):
    spec = P(("grp", "lat"), "lon", "ch")
    return jax.shard_map(
        functools.partial(on_device, mesh.shape["lat"], mesh.shape["lon"]),
        mesh=mesh,
        in_specs=(
            spec,
            P(),
            P(None, None, None, None, "ch"),
            P(None, "ch"),
            P(None, "ch", None),
            spec,
        ),
        out_specs=(spec, spec),
        check_vma=False,
    )
```

```python
import functools

import jax
import jax.numpy as jnp
from jax import lax
from jax.experimental import pallas as pl
from jax.experimental.pallas import tpu as pltpu
from jax.sharding import PartitionSpec as P

BRANCHES = 5
RMAX = 21
PADL = 24
LANES = 128
MESH = pl.DeviceIdType.MESH

SIDES = ((-1, 0), (1, 0), (0, -1), (0, 1), (-1, -1), (-1, 1), (1, -1), (1, 1))


def opposite(k):
    return SIDES.index((-SIDES[k][0], -SIDES[k][1]))


def strip_rows(rows):
    return (rows * RMAX + 15) // 16 * 16


CORNER = strip_rows(RMAX)


class Where:
    def __init__(self, n_lat, n_lon):
        self.grp = lax.axis_index("grp")
        self.lon = lax.axis_index("lon")
        self.lat = lax.axis_index("lat")
        self.ch = lax.axis_index("ch")
        self.n_lat, self.n_lon = n_lat, n_lon
        self.up = self.lat > 0
        self.down = self.lat < n_lat - 1

    def sibling(self):
        return (self.grp, self.lon, self.lat, 1 - self.ch)

    def side(self, k):
        dlat, dlon = SIDES[k]
        lon = lax.rem(self.lon + dlon + self.n_lon, self.n_lon) if dlon else self.lon
        return (self.grp, lon, self.lat + dlat, self.ch)

    def when(self, k, body):
        dlat = SIDES[k][0]
        if dlat == 0:
            body()
        else:
            pl.when(self.up if dlat < 0 else self.down)(body)

    def barrier(self):
        sem = pltpu.get_barrier_semaphore()
        pl.semaphore_signal(sem, inc=1, device_id=self.sibling(), device_id_type=MESH)
        for k in range(8):
            self.when(
                k,
                lambda k=k: pl.semaphore_signal(
                    sem, inc=1, device_id=self.side(k), device_id_type=MESH
                ),
            )
        pl.semaphore_wait(
            sem, 3 + 3 * self.up.astype(jnp.int32) + 3 * self.down.astype(jnp.int32)
        )


def gather_kernel(n_lat, n_lon, rows, cols, *refs):
    owns, refs = refs[:5], refs[5:]
    pieces = refs[:8]
    fulls = refs[8:13]
    full_feat = fulls[0]
    packed = refs[13:19]
    wide, strip, send, recv, send2, recv2, local = refs[19:]
    at = Where(n_lat, n_lon)
    me = at.ch
    copies = []
    for n, (src, dst) in enumerate(zip(owns, fulls)):
        copies.append(pltpu.make_async_copy(src, dst.at[me], local.at[n]))
        copies[-1].start()
    at.barrier()
    copies[0].wait()

    def source(k):
        dlat, dlon = SIDES[k]
        if dlon:
            return packed[k - 2]
        own = full_feat.at[me]
        return own.at[pl.ds(0, RMAX)] if dlat < 0 else own.at[pl.ds(rows - RMAX, RMAX)]

    def to_side(k):
        return pltpu.make_async_remote_copy(
            source(k),
            pieces[opposite(k)].at[me],
            send.at[k],
            recv.at[opposite(k)],
            device_id=at.side(k),
            device_id_type=MESH,
        )

    def forward(k):
        return pltpu.make_async_remote_copy(
            pieces[k].at[me],
            pieces[k].at[me],
            send2.at[k],
            recv2.at[k],
            device_id=at.sibling(),
            device_id_type=MESH,
        )

    for k in (0, 1):
        at.when(k, lambda k=k: to_side(k).start())
    wide[...] = full_feat[me].astype(jnp.float32)
    far = (rows - RMAX) * RMAX
    strip[...] = jnp.zeros_like(strip)
    for s, lo in ((0, 0), (1, cols - RMAX)):
        for n in range(rows):
            strip[s, n * RMAX : (n + 1) * RMAX, :] = wide[n, lo : lo + RMAX, :]
        for k in (2 + s, 4 + s, 6 + s):
            start, size = {2: (0, strip.shape[1]), 4: (0, CORNER), 6: (far, CORNER)}[k - s]
            packed[k - 2][...] = strip[s, start : start + size, :].astype(jnp.bfloat16)
            at.when(k, lambda k=k: to_side(k).start())
    own = []
    for n, full in enumerate(fulls):
        if n:
            copies[n].wait()
        own.append(
            pltpu.make_async_remote_copy(
                full.at[me],
                full.at[me],
                send2.at[8 + n],
                recv2.at[8 + n],
                device_id=at.sibling(),
                device_id_type=MESH,
            )
        )
        own[-1].start()

    def arrive(k):
        pltpu.make_async_remote_copy(
            pieces[k].at[me],
            pieces[k].at[me],
            send.at[k],
            recv.at[k],
            device_id=at.sibling(),
            device_id_type=MESH,
        ).wait_recv()
        forward(k).start()

    for k in (2, 3, 0, 1, 4, 5, 6, 7):
        at.when(k, lambda k=k: arrive(k))

    def other_arrives(k):
        pltpu.make_async_remote_copy(
            pieces[k].at[1 - me],
            pieces[k].at[1 - me],
            send2.at[k],
            recv2.at[k],
            device_id=at.sibling(),
            device_id_type=MESH,
        ).wait_recv()
        forward(k).wait_send()
        to_side(k).wait_send()

    for k in range(8):
        at.when(k, lambda k=k: other_arrives(k))
    for n, dst in enumerate(fulls):
        own[n].wait_send()
        pltpu.make_async_remote_copy(
            dst.at[1 - me],
            dst.at[1 - me],
            send2.at[8 + n],
            recv2.at[8 + n],
            device_id=at.sibling(),
            device_id_type=MESH,
        ).wait_recv()


def head_kernel(
    rows, cols, n_lat, info, weight, bias, merge, feat, cot, p0, p1, p2, p3, p4, p5, p6, p7,
    m_out, c_out, g0, g1, g2, g3, g4, g5, g6, g7, padded, total, merged, strip,
):
    b = pl.program_id(0)
    pieces = (p0, p1, p2, p3, p4, p5, p6, p7)
    grads = (g0, g1, g2, g3, g4, g5, g6, g7)
    all_rows = rows + 2 * RMAX
    lat = lax.axis_index("lat")
    first_row = lax.axis_index("ch") * (rows // 2)
    has_up, has_down = lat > 0, lat < n_lat - 1
    right_col = PADL + cols

    @pl.when(b == 0)
    def _():
        for c in range(2):
            padded[c, RMAX : RMAX + rows, PADL:right_col, :] = feat[c].astype(jnp.float32)
            for k in range(8):
                dlat, dlon = SIDES[k]
                top = {-1: 0, 0: RMAX, 1: RMAX + rows}[dlat]
                count = rows if dlat == 0 else RMAX
                if dlon == 0:
                    lo, hi = PADL, right_col
                elif dlon < 0:
                    lo, hi = PADL - RMAX, PADL
                else:
                    lo, hi = right_col, right_col + RMAX

                def fill(k=k, c=c, top=top, count=count, lo=lo, hi=hi, dlat=dlat, dlon=dlon):
                    if dlon == 0:
                        padded[c, top : top + count, lo:hi, :] = pieces[k][c].astype(jnp.float32)
                    else:
                        size = CORNER if dlat else strip.shape[0]
                        strip[0:size, :] = pieces[k][c].astype(jnp.float32)
                        for n in range(count):
                            start = n * RMAX
                            padded[c, top + n, lo:hi, :] = strip[start : start + RMAX, :]

                if dlat == 0:
                    fill()
                else:
                    there = has_up if dlat < 0 else has_down
                    pl.when(there)(fill)

                    @pl.when(jnp.logical_not(there))
                    def _(c=c, top=top, count=count, lo=lo, hi=hi):
                        padded[c, top : top + count, lo:hi, :] = jnp.zeros(
                            (count, hi - lo, LANES), jnp.float32
                        )
        total[...] = jnp.zeros_like(total)
        merged[...] = jnp.zeros_like(merged)

    rate = info[b]
    own_rows = rows // 2
    cells = own_rows * cols
    taps = []
    for i in range(3):
        for j in range(3):
            for c in range(2):
                tap = padded[
                    c,
                    pl.ds(first_row + RMAX + rate * (i - 1), own_rows),
                    pl.ds(PADL + rate * (j - 1), cols),
                    :,
                ]
                taps.append(tap.reshape(cells, LANES).astype(jnp.bfloat16))
    kernel = jnp.concatenate(
        [weight[h, b].reshape(9 * 2 * LANES, LANES) for h in range(2)], axis=1
    )
    preact = jnp.dot(
        jnp.concatenate(taps, axis=1), kernel, preferred_element_type=jnp.float32
    )
    preact = preact + jnp.concatenate([bias[h, pl.ds(b, 1), :] for h in range(2)], axis=1)
    sigma = 1.0 / (1.0 + jnp.exp(-preact))
    activated = (preact * sigma).astype(jnp.bfloat16)
    project = jnp.concatenate([merge[h, b] for h in range(2)], axis=0)
    here = pl.ds(pl.multiple_of(first_row * cols, cells), cells)
    merged[here, :] += jnp.dot(activated, project, preferred_element_type=jnp.float32)
    own_cot = jnp.concatenate(
        [cot[c, pl.ds(first_row, own_rows)].reshape(cells, LANES) for c in range(2)], axis=1
    )
    transposed = (((1,), (1,)), ((), ()))
    dact = lax.dot_general(own_cot, project, transposed, preferred_element_type=jnp.float32)
    dpre = (dact * (sigma * (1.0 + preact * (1.0 - sigma)))).astype(jnp.bfloat16)
    for i in range(3):
        for j in range(3):
            part = lax.dot_general(
                dpre,
                jnp.concatenate([weight[h, b, i, j] for h in range(2)], axis=1),
                transposed,
                preferred_element_type=jnp.float32,
            )
            for c in range(2):
                total[
                    c,
                    pl.ds(first_row + RMAX + rate * (i - 1), own_rows),
                    pl.ds(PADL + rate * (j - 1), cols),
                    :,
                ] += part[:, c * LANES : (c + 1) * LANES].reshape(own_rows, cols, LANES)

    @pl.when(b == BRANCHES - 1)
    def _():
        for c in range(2):
            m_out[c] = (
                merged[:, c * LANES : (c + 1) * LANES]
                .astype(jnp.bfloat16)
                .reshape(rows, cols, LANES)
            )
            c_out[c] = total[c, RMAX : RMAX + rows, PADL:right_col, :].astype(jnp.bfloat16)
            for k in range(8):
                dlat, dlon = SIDES[k]
                top = {-1: 0, 0: RMAX, 1: RMAX + rows}[dlat]
                count = rows if dlat == 0 else RMAX
                if dlon == 0:
                    grads[k][c] = total[c, top : top + count, PADL:right_col, :].astype(
                        jnp.bfloat16
                    )
                    continue
                lo = PADL - RMAX if dlon < 0 else right_col
                strip[...] = jnp.zeros_like(strip)
                for n in range(count):
                    start = n * RMAX
                    strip[start : start + RMAX, :] = total[c, top + n, lo : lo + RMAX, :]
                size = CORNER if dlat else strip.shape[0]
                grads[k][c] = strip[0:size, :].astype(jnp.bfloat16)


def scatter_kernel(n_lat, n_lon, rows, cols, m_part, c_part, *refs):
    parts = refs[:8]
    m_out, g_out = refs[8:10]
    from_sib = refs[10:18]
    staged = refs[18:26]
    landed = refs[26:34]
    m_sib, c_sib, acc, strip, send, recv, send2, recv2 = refs[34:]
    at = Where(n_lat, n_lon)
    me = at.ch
    at.barrier()

    def to_sibling(src, dst, n):
        return pltpu.make_async_remote_copy(
            src.at[1 - me], dst, send2.at[n], recv2.at[n],
            device_id=at.sibling(), device_id_type=MESH,
        )

    def to_side(k):
        return pltpu.make_async_remote_copy(
            staged[k], landed[opposite(k)], send.at[k], recv.at[opposite(k)],
            device_id=at.side(k), device_id_type=MESH,
        )

    order = (4, 5, 6, 7, 0, 1, 2, 3)
    for k in order:
        at.when(k, lambda k=k: to_sibling(parts[k], from_sib[k], k).start())
    to_sibling(c_part, c_sib, 8).start()
    to_sibling(m_part, m_sib, 9).start()

    def reduce_and_send(k):
        to_sibling(parts[k], from_sib[k], k).wait()
        staged[k][...] = (
            parts[k][me].astype(jnp.float32) + from_sib[k][...].astype(jnp.float32)
        ).astype(jnp.bfloat16)
        to_side(k).start()

    for k in order:
        at.when(k, lambda k=k: reduce_and_send(k))

    to_sibling(c_part, c_sib, 8).wait()
    acc[...] = c_part[me].astype(jnp.float32) + c_sib[...].astype(jnp.float32)
    to_sibling(m_part, m_sib, 9).wait()
    m_out[...] = (m_part[me].astype(jnp.float32) + m_sib[...].astype(jnp.float32)).astype(
        jnp.bfloat16
    )

    def arrive(k):
        dlat, dlon = SIDES[k]
        to_side(k).wait_send()
        pltpu.make_async_remote_copy(
            landed[k], landed[k], send.at[k], recv.at[k],
            device_id=at.sibling(), device_id_type=MESH,
        ).wait_recv()
        got = landed[k][...].astype(jnp.float32)
        if dlon:
            start = (rows - RMAX) * RMAX if dlat > 0 else 0
            strip[(dlon + 1) // 2, start : start + got.shape[0], :] += got
        elif dlat < 0:
            acc[0:RMAX] += got
        else:
            acc[rows - RMAX : rows] += got

    strip[...] = jnp.zeros_like(strip)
    for k in order:
        at.when(k, lambda k=k: arrive(k))
    for s, lo in ((0, 0), (1, cols - RMAX)):
        for n in range(rows):
            acc[n, lo : lo + RMAX, :] += strip[s, n * RMAX : (n + 1) * RMAX, :]
    g_out[...] = acc[...].astype(jnp.bfloat16)


def on_device(n_lat, n_lon, features, dilation_rates, branch_weight, branch_bias, merge_weight, cotangent):
    rows, cols, lanes = features.shape
    channels = merge_weight.shape[2]
    flat = strip_rows(rows)
    bf16, f32 = jnp.bfloat16, jnp.float32
    vmem = pl.BlockSpec(memory_space=pltpu.VMEM)
    hbm = pl.BlockSpec(memory_space=pltpu.HBM)

    def piece(k):
        dlat, dlon = SIDES[k]
        if dlon == 0:
            return (RMAX, cols, lanes)
        return (CORNER if dlat else flat, lanes)

    tile = jax.ShapeDtypeStruct((2, rows, cols, lanes), bf16)
    piece_pairs = [jax.ShapeDtypeStruct((2,) + piece(k), bf16) for k in range(8)]
    own = tuple(
        pltpu.with_memory_space_constraint(a, pltpu.HBM)
        for a in (features, cotangent, branch_weight, merge_weight, branch_bias)
    )
    gathered = pl.pallas_call(
        functools.partial(gather_kernel, n_lat, n_lon, rows, cols),
        out_shape=piece_pairs + [jax.ShapeDtypeStruct((2,) + a.shape, a.dtype) for a in own],
        in_specs=[hbm] * 5,
        out_specs=[vmem] * 13,
        scratch_shapes=[pltpu.VMEM(piece(k), bf16) for k in range(2, 8)]
        + [
            pltpu.VMEM((rows, cols, lanes), f32),
            pltpu.VMEM((2, flat, lanes), f32),
            pltpu.SemaphoreType.DMA((8,)),
            pltpu.SemaphoreType.DMA((8,)),
            pltpu.SemaphoreType.DMA((13,)),
            pltpu.SemaphoreType.DMA((13,)),
            pltpu.SemaphoreType.DMA((5,)),
        ],
        compiler_params=pltpu.CompilerParams(
            collective_id=0, has_side_effects=True, vmem_limit_bytes=24 * 2**20
        ),
        name="gather_halo",
    )(*own)
    pieces, full_feat, full_cot = gathered[:8], gathered[8], gathered[9]
    weights, merges, biases = gathered[10:]

    pad_cols = PADL + cols + 24
    padded_shape = (2, rows + 2 * RMAX, pad_cols, lanes)

    outs = [tile, tile] + piece_pairs
    head = pl.pallas_call(
        functools.partial(head_kernel, rows, cols, n_lat),
        out_shape=outs,
        grid_spec=pltpu.PrefetchScalarGridSpec(
            num_scalar_prefetch=1,
            grid=(BRANCHES,),
            in_specs=[vmem] * 13,
            out_specs=[vmem] * 10,
            scratch_shapes=[
                pltpu.VMEM(padded_shape, f32),
                pltpu.VMEM(padded_shape, f32),
                pltpu.VMEM((rows * cols, channels), f32),
                pltpu.VMEM((flat, lanes), f32),
            ],
        ),
        compiler_params=pltpu.CompilerParams(vmem_limit_bytes=32 * 2**20),
        name="head",
    )(
        pltpu.with_memory_space_constraint(dilation_rates, pltpu.HBM),
        weights,
        biases,
        merges,
        full_feat,
        full_cot,
        *pieces,
    )

    single = [pltpu.VMEM(piece(k), bf16) for k in range(8)]
    out = jax.ShapeDtypeStruct((rows, cols, lanes), bf16)
    return pl.pallas_call(
        functools.partial(scatter_kernel, n_lat, n_lon, rows, cols),
        out_shape=[out, out],
        in_specs=[vmem] * 10,
        out_specs=[vmem] * 2,
        scratch_shapes=single
        + single
        + single
        + [
            pltpu.VMEM((rows, cols, lanes), bf16),
            pltpu.VMEM((rows, cols, lanes), bf16),
            pltpu.VMEM((rows, cols, lanes), f32),
            pltpu.VMEM((2, flat, lanes), f32),
            pltpu.SemaphoreType.DMA((8,)),
            pltpu.SemaphoreType.DMA((8,)),
            pltpu.SemaphoreType.DMA((10,)),
            pltpu.SemaphoreType.DMA((10,)),
        ],
        compiler_params=pltpu.CompilerParams(
            collective_id=1, has_side_effects=True, vmem_limit_bytes=24 * 2**20
        ),
        name="scatter_halo",
    )(*head)


def solution(mesh):
    spec = P(("grp", "lat"), "lon", "ch")
    return jax.shard_map(
        functools.partial(on_device, mesh.shape["lat"], mesh.shape["lon"]),
        mesh=mesh,
        in_specs=(
            spec,
            P(),
            P(None, None, None, None, "ch"),
            P(None, "ch"),
            P(None, "ch", None),
            spec,
        ),
        out_specs=(spec, spec),
        check_vma=False,
    )
```

```python
import functools

import jax
import jax.numpy as jnp
from jax import lax
from jax.experimental import pallas as pl
from jax.experimental.pallas import tpu as pltpu
from jax.sharding import PartitionSpec as P

BRANCHES = 5
RMAX = 21
PADL = 24
LANES = 128
MESH = pl.DeviceIdType.MESH

SIDES = ((-1, 0), (1, 0), (0, -1), (0, 1), (-1, -1), (-1, 1), (1, -1), (1, 1))


def opposite(k):
    return SIDES.index((-SIDES[k][0], -SIDES[k][1]))


def strip_rows(rows):
    return (rows * RMAX + 15) // 16 * 16


CORNER = strip_rows(RMAX)


class Where:
    def __init__(self, n_lat, n_lon):
        self.grp = lax.axis_index("grp")
        self.lon = lax.axis_index("lon")
        self.lat = lax.axis_index("lat")
        self.ch = lax.axis_index("ch")
        self.n_lat, self.n_lon = n_lat, n_lon
        self.up = self.lat > 0
        self.down = self.lat < n_lat - 1

    def sibling(self):
        return (self.grp, self.lon, self.lat, 1 - self.ch)

    def side(self, k):
        dlat, dlon = SIDES[k]
        lon = lax.rem(self.lon + dlon + self.n_lon, self.n_lon) if dlon else self.lon
        return (self.grp, lon, self.lat + dlat, self.ch)

    def when(self, k, body):
        dlat = SIDES[k][0]
        if dlat == 0:
            body()
        else:
            pl.when(self.up if dlat < 0 else self.down)(body)

    def barrier(self):
        sem = pltpu.get_barrier_semaphore()
        pl.semaphore_signal(sem, inc=1, device_id=self.sibling(), device_id_type=MESH)
        for k in range(8):
            self.when(
                k,
                lambda k=k: pl.semaphore_signal(
                    sem, inc=1, device_id=self.side(k), device_id_type=MESH
                ),
            )
        pl.semaphore_wait(
            sem, 3 + 3 * self.up.astype(jnp.int32) + 3 * self.down.astype(jnp.int32)
        )


def gather_kernel(n_lat, n_lon, rows, cols, *refs):
    owns, refs = refs[:5], refs[5:]
    pieces = refs[:8]
    fulls = refs[8:13]
    full_feat = fulls[0]
    packed = refs[13:19]
    wide, strip, send, recv, send2, recv2, local = refs[19:]
    at = Where(n_lat, n_lon)
    me = at.ch
    copies = []
    for n, (src, dst) in enumerate(zip(owns, fulls)):
        copies.append(pltpu.make_async_copy(src, dst.at[me], local.at[n]))
        copies[-1].start()
    at.barrier()
    copies[0].wait()

    def source(k):
        dlat, dlon = SIDES[k]
        if dlon:
            return packed[k - 2]
        own = full_feat.at[me]
        return own.at[pl.ds(0, RMAX)] if dlat < 0 else own.at[pl.ds(rows - RMAX, RMAX)]

    def to_side(k):
        return pltpu.make_async_remote_copy(
            source(k),
            pieces[opposite(k)].at[me],
            send.at[k],
            recv.at[opposite(k)],
            device_id=at.side(k),
            device_id_type=MESH,
        )

    def forward(k):
        return pltpu.make_async_remote_copy(
            pieces[k].at[me],
            pieces[k].at[me],
            send2.at[k],
            recv2.at[k],
            device_id=at.sibling(),
            device_id_type=MESH,
        )

    for k in (0, 1):
        at.when(k, lambda k=k: to_side(k).start())
    wide[...] = full_feat[me].astype(jnp.float32)
    far = (rows - RMAX) * RMAX
    strip[...] = jnp.zeros_like(strip)
    for s, lo in ((0, 0), (1, cols - RMAX)):
        for n in range(rows):
            strip[s, n * RMAX : (n + 1) * RMAX, :] = wide[n, lo : lo + RMAX, :]
        for k in (2 + s, 4 + s, 6 + s):
            start, size = {2: (0, strip.shape[1]), 4: (0, CORNER), 6: (far, CORNER)}[k - s]
            packed[k - 2][...] = strip[s, start : start + size, :].astype(jnp.bfloat16)
            at.when(k, lambda k=k: to_side(k).start())
    own = []
    for n, full in enumerate(fulls):
        if n:
            copies[n].wait()
        own.append(
            pltpu.make_async_remote_copy(
                full.at[me],
                full.at[me],
                send2.at[8 + n],
                recv2.at[8 + n],
                device_id=at.sibling(),
                device_id_type=MESH,
            )
        )
        own[-1].start()

    def arrive(k):
        pltpu.make_async_remote_copy(
            pieces[k].at[me],
            pieces[k].at[me],
            send.at[k],
            recv.at[k],
            device_id=at.sibling(),
            device_id_type=MESH,
        ).wait_recv()
        forward(k).start()

    for k in (2, 3, 0, 1, 4, 5, 6, 7):
        at.when(k, lambda k=k: arrive(k))

    def other_arrives(k):
        pltpu.make_async_remote_copy(
            pieces[k].at[1 - me],
            pieces[k].at[1 - me],
            send2.at[k],
            recv2.at[k],
            device_id=at.sibling(),
            device_id_type=MESH,
        ).wait_recv()
        forward(k).wait_send()
        to_side(k).wait_send()

    for k in range(8):
        at.when(k, lambda k=k: other_arrives(k))
    for n, dst in enumerate(fulls):
        own[n].wait_send()
        pltpu.make_async_remote_copy(
            dst.at[1 - me],
            dst.at[1 - me],
            send2.at[8 + n],
            recv2.at[8 + n],
            device_id=at.sibling(),
            device_id_type=MESH,
        ).wait_recv()


def head_kernel(
    rows, cols, n_lat, info, weight, bias, merge, feat, cot, p0, p1, p2, p3, p4, p5, p6, p7,
    m_out, c_out, g0, g1, g2, g3, g4, g5, g6, g7, padded, total, merged, strip,
):
    b = pl.program_id(0)
    pieces = (p0, p1, p2, p3, p4, p5, p6, p7)
    grads = (g0, g1, g2, g3, g4, g5, g6, g7)
    all_rows = rows + 2 * RMAX
    lat = lax.axis_index("lat")
    first_row = lax.axis_index("ch") * (rows // 2)
    has_up, has_down = lat > 0, lat < n_lat - 1
    right_col = PADL + cols

    @pl.when(b == 0)
    def _():
        for c in range(2):
            padded[c, RMAX : RMAX + rows, PADL:right_col, :] = feat[c].astype(jnp.float32)
            for k in range(8):
                dlat, dlon = SIDES[k]
                top = {-1: 0, 0: RMAX, 1: RMAX + rows}[dlat]
                count = rows if dlat == 0 else RMAX
                if dlon == 0:
                    lo, hi = PADL, right_col
                elif dlon < 0:
                    lo, hi = PADL - RMAX, PADL
                else:
                    lo, hi = right_col, right_col + RMAX

                def fill(k=k, c=c, top=top, count=count, lo=lo, hi=hi, dlat=dlat, dlon=dlon):
                    if dlon == 0:
                        padded[c, top : top + count, lo:hi, :] = pieces[k][c].astype(jnp.float32)
                    else:
                        size = CORNER if dlat else strip.shape[0]
                        strip[0:size, :] = pieces[k][c].astype(jnp.float32)
                        for n in range(count):
                            start = n * RMAX
                            padded[c, top + n, lo:hi, :] = strip[start : start + RMAX, :]

                if dlat == 0:
                    fill()
                else:
                    there = has_up if dlat < 0 else has_down
                    pl.when(there)(fill)

                    @pl.when(jnp.logical_not(there))
                    def _(c=c, top=top, count=count, lo=lo, hi=hi):
                        padded[c, top : top + count, lo:hi, :] = jnp.zeros(
                            (count, hi - lo, LANES), jnp.float32
                        )
        total[...] = jnp.zeros_like(total)
        merged[...] = jnp.zeros_like(merged)

    rate = info[b]
    own_rows = rows // 2
    cells = own_rows * cols
    taps = []
    for i in range(3):
        for j in range(3):
            for c in range(2):
                tap = padded[
                    c,
                    pl.ds(first_row + RMAX + rate * (i - 1), own_rows),
                    pl.ds(PADL + rate * (j - 1), cols),
                    :,
                ]
                taps.append(tap.reshape(cells, LANES).astype(jnp.bfloat16))
    kernel = jnp.concatenate(
        [weight[h, b].reshape(9 * 2 * LANES, LANES) for h in range(2)], axis=1
    )
    preact = jnp.dot(
        jnp.concatenate(taps, axis=1), kernel, preferred_element_type=jnp.float32
    )
    preact = preact + jnp.concatenate([bias[h, pl.ds(b, 1), :] for h in range(2)], axis=1)
    sigma = 1.0 / (1.0 + jnp.exp(-preact))
    activated = (preact * sigma).astype(jnp.bfloat16)
    project = jnp.concatenate([merge[h, b] for h in range(2)], axis=0)
    merged[...] += jnp.dot(activated, project, preferred_element_type=jnp.float32)
    own_cot = jnp.concatenate(
        [cot[c, pl.ds(first_row, own_rows)].reshape(cells, LANES) for c in range(2)], axis=1
    )
    transposed = (((1,), (1,)), ((), ()))
    dact = lax.dot_general(own_cot, project, transposed, preferred_element_type=jnp.float32)
    dpre = (dact * (sigma * (1.0 + preact * (1.0 - sigma)))).astype(jnp.bfloat16)
    for i in range(3):
        for j in range(3):
            part = lax.dot_general(
                dpre,
                jnp.concatenate([weight[h, b, i, j] for h in range(2)], axis=1),
                transposed,
                preferred_element_type=jnp.float32,
            )
            for c in range(2):
                total[
                    c,
                    pl.ds(first_row + RMAX + rate * (i - 1), own_rows),
                    pl.ds(PADL + rate * (j - 1), cols),
                    :,
                ] += part[:, c * LANES : (c + 1) * LANES].reshape(own_rows, cols, LANES)

    @pl.when(b == BRANCHES - 1)
    def _():
        for c in range(2):
            m_out[c] = (
                merged[:, c * LANES : (c + 1) * LANES]
                .astype(jnp.bfloat16)
                .reshape(rows // 2, cols, LANES)
            )
            c_out[c] = total[c, RMAX : RMAX + rows, PADL:right_col, :].astype(jnp.bfloat16)
            for k in range(8):
                dlat, dlon = SIDES[k]
                top = {-1: 0, 0: RMAX, 1: RMAX + rows}[dlat]
                count = rows if dlat == 0 else RMAX
                if dlon == 0:
                    grads[k][c] = total[c, top : top + count, PADL:right_col, :].astype(
                        jnp.bfloat16
                    )
                    continue
                lo = PADL - RMAX if dlon < 0 else right_col
                strip[...] = jnp.zeros_like(strip)
                for n in range(count):
                    start = n * RMAX
                    strip[start : start + RMAX, :] = total[c, top + n, lo : lo + RMAX, :]
                size = CORNER if dlat else strip.shape[0]
                grads[k][c] = strip[0:size, :].astype(jnp.bfloat16)


def scatter_kernel(n_lat, n_lon, rows, cols, m_part, c_part, *refs):
    parts = refs[:8]
    m_out, g_out = refs[8:10]
    from_sib = refs[10:18]
    staged = refs[18:26]
    landed = refs[26:34]
    c_sib, acc, strip, send, recv, send2, recv2 = refs[34:]
    at = Where(n_lat, n_lon)
    me = at.ch
    at.barrier()

    def to_sibling(src, dst, n):
        return pltpu.make_async_remote_copy(
            src.at[1 - me], dst, send2.at[n], recv2.at[n],
            device_id=at.sibling(), device_id_type=MESH,
        )

    def to_side(k):
        return pltpu.make_async_remote_copy(
            staged[k], landed[opposite(k)], send.at[k], recv.at[opposite(k)],
            device_id=at.side(k), device_id_type=MESH,
        )

    order = (4, 5, 6, 7, 0, 1, 2, 3)
    for k in order:
        at.when(k, lambda k=k: to_sibling(parts[k], from_sib[k], k).start())
    to_sibling(c_part, c_sib, 8).start()
    own_rows = pl.ds(me * (rows // 2), rows // 2)
    their_rows = pl.ds((1 - me) * (rows // 2), rows // 2)
    to_sibling(m_part, m_out.at[own_rows], 9).start()
    m_out[own_rows] = m_part[me]

    def reduce_and_send(k):
        to_sibling(parts[k], from_sib[k], k).wait()
        staged[k][...] = (
            parts[k][me].astype(jnp.float32) + from_sib[k][...].astype(jnp.float32)
        ).astype(jnp.bfloat16)
        to_side(k).start()

    for k in order:
        at.when(k, lambda k=k: reduce_and_send(k))

    to_sibling(c_part, c_sib, 8).wait()
    acc[...] = c_part[me].astype(jnp.float32) + c_sib[...].astype(jnp.float32)
    to_sibling(m_part, m_out.at[own_rows], 9).wait_send()
    to_sibling(m_part, m_out.at[their_rows], 9).wait_recv()

    def arrive(k):
        dlat, dlon = SIDES[k]
        to_side(k).wait_send()
        pltpu.make_async_remote_copy(
            landed[k], landed[k], send.at[k], recv.at[k],
            device_id=at.sibling(), device_id_type=MESH,
        ).wait_recv()
        got = landed[k][...].astype(jnp.float32)
        if dlon:
            start = (rows - RMAX) * RMAX if dlat > 0 else 0
            strip[(dlon + 1) // 2, start : start + got.shape[0], :] += got
        elif dlat < 0:
            acc[0:RMAX] += got
        else:
            acc[rows - RMAX : rows] += got

    strip[...] = jnp.zeros_like(strip)
    for k in order:
        at.when(k, lambda k=k: arrive(k))
    for s, lo in ((0, 0), (1, cols - RMAX)):
        for n in range(rows):
            acc[n, lo : lo + RMAX, :] += strip[s, n * RMAX : (n + 1) * RMAX, :]
    g_out[...] = acc[...].astype(jnp.bfloat16)


def on_device(n_lat, n_lon, features, dilation_rates, branch_weight, branch_bias, merge_weight, cotangent):
    rows, cols, lanes = features.shape
    channels = merge_weight.shape[2]
    flat = strip_rows(rows)
    bf16, f32 = jnp.bfloat16, jnp.float32
    vmem = pl.BlockSpec(memory_space=pltpu.VMEM)
    hbm = pl.BlockSpec(memory_space=pltpu.HBM)

    def piece(k):
        dlat, dlon = SIDES[k]
        if dlon == 0:
            return (RMAX, cols, lanes)
        return (CORNER if dlat else flat, lanes)

    tile = jax.ShapeDtypeStruct((2, rows, cols, lanes), bf16)
    piece_pairs = [jax.ShapeDtypeStruct((2,) + piece(k), bf16) for k in range(8)]
    own = tuple(
        pltpu.with_memory_space_constraint(a, pltpu.HBM)
        for a in (features, cotangent, branch_weight, merge_weight, branch_bias)
    )
    gathered = pl.pallas_call(
        functools.partial(gather_kernel, n_lat, n_lon, rows, cols),
        out_shape=piece_pairs + [jax.ShapeDtypeStruct((2,) + a.shape, a.dtype) for a in own],
        in_specs=[hbm] * 5,
        out_specs=[vmem] * 13,
        scratch_shapes=[pltpu.VMEM(piece(k), bf16) for k in range(2, 8)]
        + [
            pltpu.VMEM((rows, cols, lanes), f32),
            pltpu.VMEM((2, flat, lanes), f32),
            pltpu.SemaphoreType.DMA((8,)),
            pltpu.SemaphoreType.DMA((8,)),
            pltpu.SemaphoreType.DMA((13,)),
            pltpu.SemaphoreType.DMA((13,)),
            pltpu.SemaphoreType.DMA((5,)),
        ],
        compiler_params=pltpu.CompilerParams(
            collective_id=0, has_side_effects=True, vmem_limit_bytes=24 * 2**20
        ),
        name="gather_halo",
    )(*own)
    pieces, full_feat, full_cot = gathered[:8], gathered[8], gathered[9]
    weights, merges, biases = gathered[10:]

    pad_cols = PADL + cols + 24
    padded_shape = (2, rows + 2 * RMAX, pad_cols, lanes)

    outs = [jax.ShapeDtypeStruct((2, rows // 2, cols, lanes), bf16), tile] + piece_pairs
    head = pl.pallas_call(
        functools.partial(head_kernel, rows, cols, n_lat),
        out_shape=outs,
        grid_spec=pltpu.PrefetchScalarGridSpec(
            num_scalar_prefetch=1,
            grid=(BRANCHES,),
            in_specs=[vmem] * 13,
            out_specs=[vmem] * 10,
            scratch_shapes=[
                pltpu.VMEM(padded_shape, f32),
                pltpu.VMEM(padded_shape, f32),
                pltpu.VMEM((rows // 2 * cols, channels), f32),
                pltpu.VMEM((flat, lanes), f32),
            ],
        ),
        compiler_params=pltpu.CompilerParams(vmem_limit_bytes=32 * 2**20),
        name="head",
    )(
        pltpu.with_memory_space_constraint(dilation_rates, pltpu.HBM),
        weights,
        biases,
        merges,
        full_feat,
        full_cot,
        *pieces,
    )

    single = [pltpu.VMEM(piece(k), bf16) for k in range(8)]
    out = jax.ShapeDtypeStruct((rows, cols, lanes), bf16)
    return pl.pallas_call(
        functools.partial(scatter_kernel, n_lat, n_lon, rows, cols),
        out_shape=[out, out],
        in_specs=[vmem] * 10,
        out_specs=[vmem] * 2,
        scratch_shapes=single
        + single
        + single
        + [
            pltpu.VMEM((rows, cols, lanes), bf16),
            pltpu.VMEM((rows, cols, lanes), f32),
            pltpu.VMEM((2, flat, lanes), f32),
            pltpu.SemaphoreType.DMA((8,)),
            pltpu.SemaphoreType.DMA((8,)),
            pltpu.SemaphoreType.DMA((10,)),
            pltpu.SemaphoreType.DMA((10,)),
        ],
        compiler_params=pltpu.CompilerParams(
            collective_id=1, has_side_effects=True, vmem_limit_bytes=24 * 2**20
        ),
        name="scatter_halo",
    )(*head)


def solution(mesh):
    spec = P(("grp", "lat"), "lon", "ch")
    return jax.shard_map(
        functools.partial(on_device, mesh.shape["lat"], mesh.shape["lon"]),
        mesh=mesh,
        in_specs=(
            spec,
            P(),
            P(None, None, None, None, "ch"),
            P(None, "ch"),
            P(None, "ch", None),
            spec,
        ),
        out_specs=(spec, spec),
        check_vma=False,
    )
```
